768 devices in a mesh: wide: 48 (over z, y_lo, core), narrow: 16 (over x, y_hi).
Axes of the slice: x: 4, y: 8 (y_hi: 4, y_lo: 2; y = y_hi * 2 + y_lo), z: 12, core: 2. Of those that a mesh axis runs over, the one named last changes fastest.
Arguments:
- queries: bfloat16 [147456, 768], P(('wide', 'narrow')), may hold values from -18 to 18
- passages: bfloat16 [49152, 768], P(('wide', 'narrow')), may hold values from -6 to 6
- positive: int32 [147456], P(('wide', 'narrow')), may hold values from 0 to 1023
- negative_owners: int32 [768, 8], P(('wide', 'narrow')), may hold values from 0 to 47, as said below
Outputs:
- query_grad: float32 [147456, 768], P(('wide', 'narrow'))
- passage_grad: float32 [49152, 768], P(('wide', 'narrow'))
The draws below stay inside these ranges and needn't reach their ends.
Inputs may be any that keep to these rules, and one draw needn't show every extreme that they name: `negative_owners`: each row names 8 different groups, never the group of its own block; some groups are named far more often than others.
All inputs are finite; a program needn't handle non-finite values.
Results may differ from the reference program's by a relative error of at most 0.038.
Values may be sent and summed in bfloat16 or wider, within the bound.
No kernel may reach another device: no remote copies, remote signals or barrier semaphores. Data moves between devices by JAX's collectives and lax.ppermute only.
A program may use at most 64 MiB of HBM per device.

```python
import math
import jax
import jax.numpy as jnp
from jax import lax

D = 768
QD = 192
PD = 64
NEG = 8
G = 1024
QUERIES = 147456
PASSAGES = 49152
N_WIDE = 48
N_NARROW = 16
DEVICES = 768


def shared_passages(key):
    base = jnp.clip(jax.random.normal(key, (DEVICES, PD, D), jnp.float32), -6.0, 6.0)
    rows = jnp.arange(PD)
    result = base
    for slot in range(4):
        mixed = base[:, 2 * slot + 1]
        result = jnp.where((rows == 2 * slot + 1)[None, :, None], jnp.clip(mixed, -6.0, 6.0)[:, None, :], result)
    return result


def draw_passages(key, part):
    result = shared_passages(key)
    return result.reshape(PASSAGES, D).astype(jnp.bfloat16)


def draw_queries(key, part):
    key = jax.random.fold_in(key, 5)
    values = jnp.clip(jax.random.normal(key, (DEVICES, QD, D), jnp.float32), -6.0, 6.0)
    return values.reshape(QUERIES, D).astype(jnp.bfloat16)


def draw_negative_owners(key, part):
    key = jax.random.fold_in(key, 9)
    heat = jax.random.randint(jax.random.fold_in(key, 1), (N_WIDE,), 0, 4) * 16384
    noise = jax.random.randint(jax.random.fold_in(key, 2), (DEVICES, N_WIDE), 0, 65536)
    groups = jnp.arange(N_WIDE, dtype=jnp.int32)
    scores = (noise + heat[None, :]) * 64 + groups[None, :]
    home = jnp.arange(DEVICES, dtype=jnp.int32) // N_NARROW
    scores = jnp.where(home[:, None] == groups[None, :], -1, scores)
    chosen = lax.top_k(scores, NEG)[1]
    return chosen.astype(jnp.int32)


def set_ends(values, rng, low, top_value):
    extent = values.shape
    spot = [jax.random.randint(jax.random.fold_in(rng, axis), (), 0, extent[axis]) for axis in range(len(extent))]
    values = values.at[tuple(spot)].set(low)
    longest = extent.index(max(extent))
    spot[longest] = (spot[longest] + 1) % extent[longest]
    return values.at[tuple(spot)].set(top_value)


def setup_inputs(seed: int = 0) -> dict:
    streams_of = jax.random.split(jax.random.key(seed), 5)
    queries = draw_queries(jax.random.fold_in(streams_of[4], 71), 0)
    passages = draw_passages(jax.random.fold_in(streams_of[4], 71), 0)
    positive = set_ends(jax.random.randint(streams_of[2], (QUERIES,), 0, G), jax.random.fold_in(streams_of[2], 1), 0, G - 1).astype(jnp.int32)
    negative_owners = draw_negative_owners(jax.random.fold_in(streams_of[4], 71), 0)
    return dict(queries=queries, passages=passages, positive=positive, negative_owners=negative_owners)


def device_step(grads, device_id, query_all, passage_all, positive_all, owner_all, scaling):
    wide_id = device_id // N_NARROW
    narrow_id = device_id % N_NARROW
    query_rows = query_all[wide_id, narrow_id]
    pool = passage_all[wide_id].reshape(G, D)
    owners = owner_all[wide_id, narrow_id]
    named = passage_all[owners, narrow_id].reshape(NEG * PD, D)
    key_rows = jnp.concatenate([pool, named], axis=0)
    logits = jnp.dot(query_rows, key_rows.T, preferred_element_type=jnp.float32) * scaling
    row_max = lax.optimization_barrier(jnp.max(logits, axis=-1, keepdims=True))
    row_total = row_max + jnp.log(lax.optimization_barrier(jnp.sum(jnp.exp(logits - row_max), axis=-1, keepdims=True)))
    chances = jnp.exp(logits - row_total)
    columns = jnp.arange(G + NEG * PD, dtype=jnp.int32)
    target = (positive_all[wide_id, narrow_id][:, None] == columns[None, :]).astype(jnp.float32)
    dlogits = chances - target
    query_grad = jnp.dot(dlogits, key_rows.astype(jnp.float32), precision=lax.Precision.HIGHEST) * scaling
    key_grad = jnp.dot(dlogits.T, query_rows.astype(jnp.float32), precision=lax.Precision.HIGHEST) * scaling
    grads = grads.at[wide_id].add(key_grad[:G].reshape(N_NARROW, PD, D))
    grads = grads.at[owners, narrow_id].add(key_grad[G:].reshape(NEG, PD, D))
    return (grads, query_grad)

def reference(queries, passages, positive, negative_owners):
    scaling = 4.0 / math.sqrt(D)
    query_all = queries.reshape(N_WIDE, N_NARROW, QD, D)
    passage_all = passages.reshape(N_WIDE, N_NARROW, PD, D)
    positive_all = positive.reshape(N_WIDE, N_NARROW, QD)
    owner_all = negative_owners.reshape(N_WIDE, N_NARROW, NEG)
    start_grads = jnp.zeros((N_WIDE, N_NARROW, PD, D), jnp.float32)

    def step_fn(grads, device_id):
        return device_step(grads, device_id, query_all, passage_all, positive_all, owner_all, scaling)
    grads, query_grads = lax.scan(step_fn, start_grads, jnp.arange(N_WIDE * N_NARROW, dtype=jnp.int32))
    return (query_grads.reshape(QUERIES, D), grads.reshape(PASSAGES, D))
```

```python
import functools
import math

import jax
import jax.numpy as jnp
from jax import lax
from jax.experimental import pallas as pl
from jax.experimental.pallas import tpu as pltpu
from jax.sharding import Mesh
from jax.sharding import PartitionSpec as P

AXES = ("zs", "zl", "yl", "c", "x", "yh")
WIDE = ("zs", "zl", "yl", "c")
RUN = ("zl", "yl", "c")
LANES = 128
SUBS = 8
LIFT = 128.0
DROP = 1.0 / 16.0
VMEM = 12 * 1024 * 1024
STEP = 256


def dot_nt(a, b):
    return lax.dot_general(a, b, (((1,), (1,)), ((), ())), preferred_element_type=jnp.float32)


def dot_tn(a, b):
    return lax.dot_general(a, b, (((0,), (0,)), ((), ())), preferred_element_type=jnp.float32)


def dot_nn(a, b):
    return lax.dot_general(a, b, (((1,), (0,)), ((), ())), preferred_element_type=jnp.float32)


def join_pieces(named_ref, keys_ref, row_tiles, col_tiles):
    rows = named_ref.shape[1]
    for r in range(row_tiles):
        for c in range(col_tiles):
            keys_ref[r * rows : (r + 1) * rows, c * LANES : (c + 1) * LANES] = named_ref[r * col_tiles + c]


def pick_kernel(run_ref, owners_ref, held_ref, out_ref):
    members, tiles, count = out_ref.shape[:3]
    stride = held_ref.shape[0] // (owners_ref.shape[0] // count)

    def body(i, carry):
        for k in range(count):
            owner = owners_ref[(run_ref[0] * members + i) * count + k]
            for u in range(tiles):
                out_ref[i, u, k] = held_ref[owner * stride + u]
        return carry

    lax.fori_loop(0, members, body, 0)


def gather_sum_kernel(run_ref, owners_ref, terms_ref, out_ref, *acc_refs):
    members, tiles, count = terms_ref.shape[:3]
    for u in range(tiles):
        acc_refs[u][...] = jnp.zeros_like(acc_refs[u])

    def body(i, carry):
        for k in range(count):
            owner = owners_ref[(run_ref[0] * members + i) * count + k]
            for u in range(tiles):
                acc_refs[u][owner] += terms_ref[i, u, k]
        return carry

    lax.fori_loop(0, members, body, 0)
    for u in range(tiles):
        out_ref[:, u] = acc_refs[u][...] * DROP


def pool_kernel(q_ref, *refs):
    slab_refs, (exp_ref, top_ref, sum_ref) = refs[:-3], refs[-3:]
    width = q_ref.shape[1]
    step = slab_refs[0].shape[0]
    scaling = 4.0 / math.sqrt(width)
    q = q_ref[...]
    top = None
    for slot, slab_ref in enumerate(slab_refs):
        part = dot_nt(q, slab_ref[...]) * scaling
        exp_ref[:, slot * step : (slot + 1) * step] = part
        high = jnp.max(part, axis=-1, keepdims=True)
        top = high if top is None else jnp.maximum(top, high)
    total = jnp.zeros_like(top)
    for slot in range(len(slab_refs)):
        part = jnp.exp(exp_ref[:, slot * step : (slot + 1) * step] - top)
        exp_ref[:, slot * step : (slot + 1) * step] = part
        total += jnp.sum(part, axis=-1, keepdims=True)
    top_ref[...] = top
    sum_ref[...] = total


def split(grad):
    hi = grad.astype(jnp.bfloat16)
    return hi, (grad - hi.astype(jnp.float32)).astype(jnp.bfloat16)


def named_kernel(q_ref, named_ref, top_ref, sum_ref, hi_ref, lo_ref, grad_ref, share_ref, keys_ref, l_ref):
    width = q_ref.shape[1]
    col_tiles = width // LANES
    row_tiles = named_ref.shape[0] // col_tiles
    piece_rows = named_ref.shape[1]
    named_rows = row_tiles * piece_rows
    scaling = 4.0 / math.sqrt(width)
    join_pieces(named_ref, keys_ref, row_tiles, col_tiles)
    q = q_ref[...]
    pool_top = top_ref[...]
    top = pool_top
    for c in range(0, named_rows, STEP):
        part = dot_nt(q, keys_ref[c : c + STEP, :]) * scaling
        l_ref[:, c : c + STEP] = part
        top = jnp.maximum(top, jnp.max(part, axis=-1, keepdims=True))
    pool_scale = jnp.exp(pool_top - top)
    total = sum_ref[...] * pool_scale
    for c in range(0, named_rows, STEP):
        part = jnp.exp(l_ref[:, c : c + STEP] - top)
        l_ref[:, c : c + STEP] = part
        total += jnp.sum(part, axis=-1, keepdims=True)
    share = 1.0 / total
    share_ref[...] = share * pool_scale
    for c in range(0, named_rows, STEP):
        hi, lo = split(l_ref[:, c : c + STEP] * share)
        hi_ref[:, c : c + STEP] = hi
        lo_ref[:, c : c + STEP] = lo
        terms = (dot_tn(hi, q) + dot_tn(lo, q)) * (scaling * LIFT)
        first = c // piece_rows
        for r in range(STEP // piece_rows):
            for k in range(col_tiles):
                grad_ref[(first + r) * col_tiles + k] = terms[
                    r * piece_rows : (r + 1) * piece_rows, k * LANES : (k + 1) * LANES
                ]


def pool_grad_kernel(q_ref, exp_ref, share_ref, pos_ref, hi_ref, lo_ref, *grad_refs):
    queries, width = q_ref.shape
    scaling = 4.0 / math.sqrt(width)
    q = q_ref[...]
    share = share_ref[...]
    across = lax.broadcasted_iota(jnp.int32, (queries, queries), 1)
    down = lax.broadcasted_iota(jnp.int32, (queries, queries), 0)
    pos = jnp.sum(jnp.where(across == down, pos_ref[...].astype(jnp.float32), 0.0), axis=1, keepdims=True)
    pos = pos.astype(jnp.int32)
    step = grad_refs[0].shape[0]
    for slot, grad_ref in enumerate(grad_refs):
        first, last = slot * step, (slot + 1) * step
        columns = lax.broadcasted_iota(jnp.int32, (queries, step), 1) + first
        hi, lo = split(exp_ref[:, first:last] * share - (columns == pos).astype(jnp.float32))
        hi_ref[:, first:last] = hi
        lo_ref[:, first:last] = lo
        grad_ref[...] = (dot_tn(hi, q) + dot_tn(lo, q)) * (scaling * LIFT)


def query_kernel(pool_hi_ref, pool_lo_ref, hi_ref, lo_ref, named_ref, *refs):
    slab_refs, out_ref, keys_ref = refs[:-2], refs[-2], refs[-1]
    step, width = slab_refs[0].shape
    col_tiles = width // LANES
    row_tiles = named_ref.shape[0] // col_tiles
    scaling = 4.0 / math.sqrt(width)
    join_pieces(named_ref, keys_ref, row_tiles, col_tiles)
    total = dot_nn(hi_ref[...], keys_ref[...]) + dot_nn(lo_ref[...], keys_ref[...])
    for slot, slab_ref in enumerate(slab_refs):
        first, last = slot * step, (slot + 1) * step
        total += dot_nn(pool_hi_ref[:, first:last], slab_ref[...])
        total += dot_nn(pool_lo_ref[:, first:last], slab_ref[...])
    out_ref[...] = total * scaling


def call(kernel, outs, scratch, flops, *args, smem=0, after=()):
    vmem = pl.BlockSpec(memory_space=pltpu.VMEM)
    specs = [pl.BlockSpec(memory_space=pltpu.SMEM)] * smem + [vmem] * (len(args) - smem)
    specs += [pl.BlockSpec(memory_space=pltpu.HBM)] * len(after)
    count = len(args)

    def body(*refs):
        kernel(*refs[:count], *refs[count + len(after) :])

    return pl.pallas_call(
        body,
        out_shape=tuple(jax.ShapeDtypeStruct(shape, dtype) for shape, dtype in outs),
        in_specs=specs,
        out_specs=(vmem,) * len(outs),
        scratch_shapes=scratch,
        compiler_params=pltpu.CompilerParams(vmem_limit_bytes=VMEM),
        cost_estimate=pl.CostEstimate(flops=flops, bytes_accessed=4 * 1024 * 1024, transcendentals=0),
    )(*args, *after)


def local(queries, passages, positive, negative_owners):
    query_count, width = queries.shape
    block_rows = passages.shape[0]
    neg_count = negative_owners.shape[1]
    f32, bf16, half = jnp.float32, jnp.bfloat16, jnp.float16
    wide, members, runs = lax.axis_size(WIDE), lax.axis_size(RUN), lax.axis_size("zs")
    near, far = lax.axis_size("yh"), lax.axis_size("x")
    row_tiles, col_tiles = block_rows // SUBS, width // LANES
    tiles = row_tiles * col_tiles // members
    pool_rows = far * near * block_rows
    named_rows = neg_count * block_rows
    swaps = [[(i, i ^ k) for i in range(near)] for k in range(near)]
    here_x, here_y = lax.axis_index("x"), lax.axis_index("yh")
    run = lax.axis_index("zs").astype(jnp.int32)[None]

    pieces = passages.reshape(row_tiles, SUBS, col_tiles, LANES).transpose(0, 2, 1, 3)
    pieces = pieces.reshape(members, tiles * SUBS, LANES)
    names = jnp.zeros((SUBS, LANES), bf16).at[0, :neg_count].set(negative_owners[0].astype(bf16))
    sent = jnp.concatenate([pieces, jnp.broadcast_to(names[None], (members, SUBS, LANES))], axis=1)
    sent = jnp.broadcast_to(sent[None], (runs,) + sent.shape).reshape((wide,) + sent.shape[1:])
    with jax.named_scope("spread_pieces"):
        spread = lax.all_to_all(sent, WIDE, 0, 0, tiled=True)
    owners = spread[:, tiles * SUBS, :neg_count].astype(jnp.int32).reshape(wide * neg_count)

    with jax.named_scope("pool_yh"):
        mine = [passages] + [lax.ppermute(passages, "yh", swaps[k]) for k in range(1, near)]
    with jax.named_scope("pool_x"):
        mine = jnp.concatenate(mine, axis=0)
        slabs = [mine] + [lax.ppermute(mine, "x", swaps[k]) for k in range(1, far)]
    slots = positive ^ ((here_x * near + here_y) * block_rows)

    (picked,) = call(
        pick_kernel,
        [((members, tiles, neg_count, SUBS, LANES), bf16)],
        [],
        0,
        run,
        owners,
        spread.reshape(wide * (tiles + 1), SUBS, LANES),
        smem=2,
        after=(mine,),
    )
    with jax.named_scope("named_pieces"):
        named = lax.all_to_all(picked, RUN, 0, 0, tiled=True)
    named = named.reshape(members * tiles, neg_count * SUBS, LANES)

    product = 2 * query_count * width
    exps, top, total = call(
        pool_kernel,
        [((query_count, pool_rows), f32), ((query_count, 1), f32), ((query_count, 1), f32)],
        [],
        product * pool_rows,
        queries,
        *slabs,
    )
    named_hi, named_lo, named_grad, share = call(
        named_kernel,
        [
            ((query_count, named_rows), bf16),
            ((query_count, named_rows), bf16),
            ((members * tiles, neg_count * SUBS, LANES), f32),
            ((query_count, 1), f32),
        ],
        [pltpu.VMEM((named_rows, width), bf16), pltpu.VMEM((query_count, named_rows), f32)],
        3 * product * named_rows,
        queries,
        named,
        top,
        total,
    )
    with jax.named_scope("named_back"):
        back = named_grad.astype(half).reshape(members, tiles, neg_count, SUBS, LANES)
        back = lax.all_to_all(back, RUN, 0, 0, tiled=True)

    pool_hi, pool_lo, *pool_grads = call(
        pool_grad_kernel,
        [((query_count, pool_rows), bf16)] * 2 + [((near * block_rows, width), f32)] * far,
        [],
        2 * product * pool_rows,
        queries,
        exps,
        share,
        slots[None, :],
    )
    rows_x = pool_grads[0]
    leaving = [grad.astype(half) for grad in pool_grads[1:]]
    with jax.named_scope("grad_x"):
        for k in range(1, far):
            part = lax.ppermute(leaving[k - 1], "x", swaps[k])
            rows_x = rows_x + part.astype(f32)
    owned = rows_x[:block_rows]
    with jax.named_scope("grad_yh"):
        for k in range(1, near):
            part = (rows_x[k * block_rows : (k + 1) * block_rows] * (1.0 / far)).astype(half)
            part = lax.ppermute(part, "yh", swaps[k])
            owned = owned + part.astype(f32) * float(far)

    (query_grad,) = call(
        query_kernel,
        [((query_count, width), f32)],
        [pltpu.VMEM((named_rows, width), bf16)],
        30 * product * (pool_rows + named_rows),
        pool_hi,
        pool_lo,
        named_hi,
        named_lo,
        named,
        *slabs,
    )

    (summed,) = call(
        gather_sum_kernel,
        [((wide, tiles, SUBS, LANES), f32)],
        [pltpu.VMEM((wide, SUBS, LANES), f32)] * tiles,
        0,
        run,
        owners,
        back.astype(f32),
        smem=2,
        after=tuple(pool_grads[1:]),
    )
    with jax.named_scope("pieces_home"):
        home = lax.all_to_all(summed.astype(half), WIDE, 0, 0, tiled=True)
    home = home.astype(f32).reshape(runs, row_tiles, col_tiles, SUBS, LANES)
    returned = home.sum(0).transpose(0, 2, 1, 3).reshape(block_rows, width)
    return (query_grad, owned * (1.0 / LIFT) + returned * (1.0 / (LIFT * DROP)))


def solution(mesh):
    whole = Mesh(mesh.devices.reshape(4, 3, 2, 2, 4, 4), AXES)
    spec = P(AXES, None)
    return jax.shard_map(
        local,
        mesh=whole,
        in_specs=(spec, spec, P(AXES), spec),
        out_specs=(spec, spec),
        check_vma=False,
    )
```

```python
import functools
import math

import jax
import jax.numpy as jnp
from jax import lax
from jax.experimental import pallas as pl
from jax.experimental.pallas import tpu as pltpu
from jax.sharding import Mesh
from jax.sharding import PartitionSpec as P

AXES = ("zs", "zl", "yl", "c", "x", "yh")
WIDE = ("zs", "zl", "yl", "c")
RUN = ("zl", "yl", "c")
LANES = 128
SUBS = 8
LIFT = 128.0
DROP = 1.0 / 16.0
VMEM = 16 * 1024 * 1024
STEP = 256


def dot_nt(a, b):
    return lax.dot_general(a, b, (((1,), (1,)), ((), ())), preferred_element_type=jnp.float32)


def dot_tn(a, b):
    return lax.dot_general(a, b, (((0,), (0,)), ((), ())), preferred_element_type=jnp.float32)


def dot_nn(a, b):
    return lax.dot_general(a, b, (((1,), (0,)), ((), ())), preferred_element_type=jnp.float32)


def join_pieces(named_ref, keys_ref, row_tiles, col_tiles):
    rows = named_ref.shape[1]
    for r in range(row_tiles):
        for c in range(col_tiles):
            keys_ref[r * rows : (r + 1) * rows, c * LANES : (c + 1) * LANES] = named_ref[r * col_tiles + c]


def pick_kernel(run_ref, owners_ref, held_ref, out_ref):
    members, tiles, count = out_ref.shape[:3]
    stride = held_ref.shape[0] // (owners_ref.shape[0] // count)

    first = run_ref[0] * members
    for i in range(members):
        for k in range(count):
            owner = owners_ref[(first + i) * count + k]
            for u in range(tiles):
                out_ref[i, u, k] = held_ref[owner * stride + u]


def gather_sum_kernel(run_ref, owners_ref, terms_ref, out_ref, *acc_refs):
    members, tiles, count = terms_ref.shape[:3]
    for u in range(tiles):
        acc_refs[u][...] = jnp.zeros_like(acc_refs[u])

    def body(i, carry):
        for k in range(count):
            owner = owners_ref[(run_ref[0] * members + i) * count + k]
            for u in range(tiles):
                acc_refs[u][owner] += terms_ref[i, u, k]
        return carry

    lax.fori_loop(0, members, body, 0)
    for u in range(tiles):
        out_ref[:, u] = acc_refs[u][...] * DROP


def pool_kernel(q_ref, *refs):
    slab_refs, exp_ref = refs[:-1], refs[-1]
    width = q_ref.shape[1]
    step = slab_refs[0].shape[0]
    scaling = 4.0 / math.sqrt(width)
    q = q_ref[...]
    top = None
    for slot, slab_ref in enumerate(slab_refs):
        part = dot_nt(q, slab_ref[...]) * scaling
        exp_ref[:, slot * step : (slot + 1) * step] = part
        high = jnp.max(part, axis=-1, keepdims=True)
        top = high if top is None else jnp.maximum(top, high)
    total = jnp.zeros_like(top)
    for slot in range(len(slab_refs)):
        part = jnp.exp(exp_ref[:, slot * step : (slot + 1) * step] - top)
        exp_ref[:, slot * step : (slot + 1) * step] = part
        total += jnp.sum(part, axis=-1, keepdims=True)
    last = step * len(slab_refs)
    exp_ref[:, last : last + LANES] = jnp.broadcast_to(top, (q.shape[0], LANES))
    exp_ref[:, last + LANES : last + 2 * LANES] = jnp.broadcast_to(total, (q.shape[0], LANES))
    exp_ref[:, last + 2 * LANES :] = q.astype(jnp.float32)


def split(grad):
    hi = grad.astype(jnp.bfloat16)
    return hi, (grad - hi.astype(jnp.float32)).astype(jnp.bfloat16)


def grads_kernel(place_ref, named_ref, exp_ref, pos_ref, hi_ref, lo_ref, named_out, *refs):
    grad_refs, (keys_ref, l_ref) = refs[:-2], refs[-2:]
    queries, width = exp_ref.shape[0], keys_ref.shape[1]
    col_tiles = width // LANES
    row_tiles = named_ref.shape[0] // col_tiles
    piece_rows = named_ref.shape[1]
    named_rows = row_tiles * piece_rows
    step = grad_refs[0].shape[0]
    pool_rows = step * len(grad_refs)
    scaling = 4.0 / math.sqrt(width)
    join_pieces(named_ref, keys_ref, row_tiles, col_tiles)
    q = exp_ref[:, pool_rows + 2 * LANES :].astype(jnp.bfloat16)
    pool_top = exp_ref[:, pool_rows : pool_rows + 1]
    top = pool_top
    for c in range(0, named_rows, STEP):
        part = dot_nt(q, keys_ref[c : c + STEP, :]) * scaling
        l_ref[:, c : c + STEP] = part
        top = jnp.maximum(top, jnp.max(part, axis=-1, keepdims=True))
    pool_scale = jnp.exp(pool_top - top)
    total = exp_ref[:, pool_rows + LANES : pool_rows + LANES + 1] * pool_scale
    for c in range(0, named_rows, STEP):
        part = jnp.exp(l_ref[:, c : c + STEP] - top)
        l_ref[:, c : c + STEP] = part
        total += jnp.sum(part, axis=-1, keepdims=True)
    share = 1.0 / total
    for c in range(0, named_rows, STEP):
        hi, lo = split(l_ref[:, c : c + STEP] * share)
        hi_ref[:, pool_rows + c : pool_rows + c + STEP] = hi
        lo_ref[:, pool_rows + c : pool_rows + c + STEP] = lo
        terms = (dot_tn(hi, q) + dot_tn(lo, q)) * (scaling * LIFT)
        first = c // piece_rows
        for r in range(STEP // piece_rows):
            for k in range(col_tiles):
                named_out[(first + r) * col_tiles + k] = terms[
                    r * piece_rows : (r + 1) * piece_rows, k * LANES : (k + 1) * LANES
                ]

    across = lax.broadcasted_iota(jnp.int32, (queries, queries), 1)
    down = lax.broadcasted_iota(jnp.int32, (queries, queries), 0)
    pos = jnp.sum(jnp.where(across == down, pos_ref[...].astype(jnp.float32), 0.0), axis=1, keepdims=True)
    pos = pos.astype(jnp.int32)
    share = share * pool_scale
    block = step // place_ref.shape[0]
    for slot, grad_ref in enumerate(grad_refs):
        first, last = slot * step, (slot + 1) * step
        columns = lax.broadcasted_iota(jnp.int32, (queries, step), 1) + first
        hi, lo = split(exp_ref[:, first:last] * share - (columns == pos).astype(jnp.float32))
        hi_ref[:, first:last] = hi
        lo_ref[:, first:last] = lo
        terms = (dot_tn(hi, q) + dot_tn(lo, q)) * (scaling * LIFT)
        for r in range(step // block):
            grad_ref[pl.ds(pl.multiple_of(place_ref[r] * block, block), block), :] = terms[r * block : (r + 1) * block]


def query_kernel(hi_ref, lo_ref, named_ref, *refs):
    slab_refs, out_ref, keys_ref = refs[:-2], refs[-2], refs[-1]
    step, width = slab_refs[0].shape
    col_tiles = width // LANES
    row_tiles = named_ref.shape[0] // col_tiles
    pool_rows = step * len(slab_refs)
    scaling = 4.0 / math.sqrt(width)
    join_pieces(named_ref, keys_ref, row_tiles, col_tiles)
    total = dot_nn(hi_ref[:, pool_rows:], keys_ref[...]) + dot_nn(lo_ref[:, pool_rows:], keys_ref[...])
    for slot, slab_ref in enumerate(slab_refs):
        first, last = slot * step, (slot + 1) * step
        total += dot_nn(hi_ref[:, first:last], slab_ref[...])
        total += dot_nn(lo_ref[:, first:last], slab_ref[...])
    out_ref[...] = total * scaling


def call(kernel, outs, scratch, flops, *args, smem=0, after=()):
    vmem = pl.BlockSpec(memory_space=pltpu.VMEM)
    specs = [pl.BlockSpec(memory_space=pltpu.SMEM)] * smem + [vmem] * (len(args) - smem)
    specs += [pl.BlockSpec(memory_space=pltpu.HBM)] * len(after)
    count = len(args)

    def body(*refs):
        kernel(*refs[:count], *refs[count + len(after) :])

    return pl.pallas_call(
        body,
        out_shape=tuple(jax.ShapeDtypeStruct(shape, dtype) for shape, dtype in outs),
        in_specs=specs,
        out_specs=(vmem,) * len(outs),
        scratch_shapes=scratch,
        compiler_params=pltpu.CompilerParams(vmem_limit_bytes=VMEM),
        cost_estimate=pl.CostEstimate(flops=flops, bytes_accessed=4 * 1024 * 1024, transcendentals=0),
    )(*args, *after)


def local(queries, passages, positive, negative_owners):
    query_count, width = queries.shape
    block_rows = passages.shape[0]
    neg_count = negative_owners.shape[1]
    f32, bf16, half = jnp.float32, jnp.bfloat16, jnp.float16
    wide, members, runs = lax.axis_size(WIDE), lax.axis_size(RUN), lax.axis_size("zs")
    near, far = lax.axis_size("yh"), lax.axis_size("x")
    row_tiles, col_tiles = block_rows // SUBS, width // LANES
    tiles = row_tiles * col_tiles // members
    pool_rows = far * near * block_rows
    named_rows = neg_count * block_rows
    swaps = [[(i, i ^ k) for i in range(near)] for k in range(near)]
    here_x, here_y = lax.axis_index("x"), lax.axis_index("yh")
    run = lax.axis_index("zs").astype(jnp.int32)[None]

    pieces = passages.reshape(row_tiles, SUBS, col_tiles, LANES).transpose(0, 2, 1, 3)
    pieces = pieces.reshape(members, tiles * SUBS, LANES)
    names = jnp.zeros((SUBS, LANES), bf16).at[0, :neg_count].set(negative_owners[0].astype(bf16))
    sent = jnp.concatenate(
        [
            jnp.broadcast_to(pieces[None], (runs,) + pieces.shape),
            jnp.broadcast_to(names[None, None], (runs, members) + names.shape),
        ],
        axis=2,
    ).reshape(wide, (tiles + 1) * SUBS, LANES)
    with jax.named_scope("spread_pieces"):
        spread = lax.all_to_all(sent, WIDE, 0, 0, tiled=True)
    owners = spread[:, tiles * SUBS, :neg_count].astype(jnp.int32).reshape(wide * neg_count)

    with jax.named_scope("pool_yh"):
        mine = lax.all_gather(passages, "yh", axis=0, tiled=True)
    with jax.named_scope("pool_x"):
        slabs = [mine] + [lax.ppermute(mine, "x", swaps[k]) for k in range(1, far)]
    slots = positive ^ (here_x * (near * block_rows))

    (picked,) = call(
        pick_kernel,
        [((members, tiles, neg_count, SUBS, LANES), bf16)],
        [],
        0,
        run,
        owners,
        spread.reshape(wide * (tiles + 1), SUBS, LANES),
        smem=2,
        after=(mine,),
    )
    with jax.named_scope("named_pieces"):
        named = lax.all_to_all(picked, RUN, 0, 0, tiled=True)
    named = named.reshape(members * tiles, neg_count * SUBS, LANES)

    product = 2 * query_count * width
    (exps,) = call(
        pool_kernel,
        [((query_count, pool_rows + 2 * LANES + width), f32)],
        [],
        100 * product * pool_rows,
        queries,
        *slabs,
    )
    total_rows = pool_rows + named_rows
    hi, lo, named_grad, *pool_grads = call(
        grads_kernel,
        [
            ((query_count, total_rows), bf16),
            ((query_count, total_rows), bf16),
            ((members * tiles, neg_count * SUBS, LANES), f32),
        ]
        + [((near * block_rows, width), f32)] * far,
        [pltpu.VMEM((named_rows, width), bf16), pltpu.VMEM((query_count, named_rows), f32)],
        2 * product * total_rows,
        jnp.arange(near, dtype=jnp.int32) ^ here_y.astype(jnp.int32),
        named,
        exps,
        slots[None, :],
        smem=1,
    )
    with jax.named_scope("named_back"):
        back = named_grad.astype(half).reshape(members, tiles, neg_count, SUBS, LANES)
        back = lax.all_to_all(back, RUN, 0, 0, tiled=True)

    rows_x = pool_grads[0]
    leaving = [grad.astype(half) for grad in pool_grads[1:]]
    with jax.named_scope("grad_x"):
        for k in range(1, far):
            part = lax.ppermute(leaving[k - 1], "x", swaps[k])
            rows_x = rows_x + part.astype(f32)
    owned = rows_x[:block_rows]
    with jax.named_scope("grad_yh"):
        for k in range(1, near):
            part = (rows_x[k * block_rows : (k + 1) * block_rows] * (1.0 / far)).astype(half)
            part = lax.ppermute(part, "yh", swaps[k])
            owned = owned + part.astype(f32) * float(far)

    (query_grad,) = call(
        query_kernel,
        [((query_count, width), f32)],
        [pltpu.VMEM((named_rows, width), bf16)],
        8 * product * (pool_rows + named_rows),
        hi,
        lo,
        named,
        *slabs,
        after=(rows_x,),
    )

    (summed,) = call(
        gather_sum_kernel,
        [((wide, tiles, SUBS, LANES), f32)],
        [pltpu.VMEM((wide, SUBS, LANES), f32)] * tiles,
        0,
        run,
        owners,
        back.astype(f32),
        smem=2,
    )
    with jax.named_scope("pieces_home"):
        home = lax.all_to_all(summed.astype(half), WIDE, 0, 0, tiled=True)
    home = home.astype(f32).reshape(runs, row_tiles, col_tiles, SUBS, LANES)
    returned = home.sum(0).transpose(0, 2, 1, 3).reshape(block_rows, width)
    return (query_grad, owned * (1.0 / LIFT) + returned * (1.0 / (LIFT * DROP)))


def solution(mesh):
    whole = Mesh(mesh.devices.reshape(4, 3, 2, 2, 4, 4), AXES)
    spec = P(AXES, None)
    return jax.shard_map(
        local,
        mesh=whole,
        in_specs=(spec, spec, P(AXES), spec),
        out_specs=(spec, spec),
        check_vma=False,
    )
```

```python
import functools
import math

import jax
import jax.numpy as jnp
from jax import lax
from jax.experimental import pallas as pl
from jax.experimental.pallas import tpu as pltpu
from jax.sharding import Mesh
from jax.sharding import PartitionSpec as P

AXES = ("zs", "zl", "yl", "c", "x", "yh")
WIDE = ("zs", "zl", "yl", "c")
RUN = ("zl", "yl", "c")
LANES = 128
SUBS = 8
LIFT = 128.0
DROP = 1.0 / 16.0
VMEM = 16 * 1024 * 1024
STEP = 256


def dot_nt(a, b):
    return lax.dot_general(a, b, (((1,), (1,)), ((), ())), preferred_element_type=jnp.float32)


def dot_tn(a, b):
    return lax.dot_general(a, b, (((0,), (0,)), ((), ())), preferred_element_type=jnp.float32)


def dot_nn(a, b):
    return lax.dot_general(a, b, (((1,), (0,)), ((), ())), preferred_element_type=jnp.float32)


def join_pieces(named_ref, keys_ref, row_tiles, col_tiles):
    rows = named_ref.shape[1]
    for r in range(row_tiles):
        for c in range(col_tiles):
            keys_ref[r * rows : (r + 1) * rows, c * LANES : (c + 1) * LANES] = named_ref[r * col_tiles + c]


def pick_kernel(run_ref, owners_ref, held_ref, out_ref):
    members, tiles, count = out_ref.shape[:3]
    stride = held_ref.shape[0] // (owners_ref.shape[0] // count)

    first = run_ref[0] * members
    for i in range(members):
        for k in range(count):
            owner = owners_ref[(first + i) * count + k]
            for u in range(tiles):
                out_ref[i, u, k] = held_ref[owner * stride + u]


def gather_sum_kernel(run_ref, owners_ref, terms_ref, out_ref, *acc_refs):
    members, tiles, count = terms_ref.shape[:3]
    for u in range(tiles):
        acc_refs[u][...] = jnp.zeros_like(acc_refs[u])

    def body(i, carry):
        for k in range(count):
            owner = owners_ref[(run_ref[0] * members + i) * count + k]
            for u in range(tiles):
                acc_refs[u][owner] += terms_ref[i, u, k]
        return carry

    lax.fori_loop(0, members, body, 0)
    for u in range(tiles):
        out_ref[:, u] = acc_refs[u][...] * DROP


def pool_kernel(q_ref, *refs):
    slab_refs, (exp_ref, stat_ref) = refs[:-2], refs[-2:]
    width = q_ref.shape[1]
    step = slab_refs[0].shape[0]
    scaling = 4.0 / math.sqrt(width)
    q = q_ref[...]
    top = None
    for slot, slab_ref in enumerate(slab_refs):
        part = dot_nt(q, slab_ref[...]) * scaling
        exp_ref[:, slot * step : (slot + 1) * step] = part
        high = jnp.max(part, axis=-1, keepdims=True)
        top = high if top is None else jnp.maximum(top, high)
    total = jnp.zeros_like(top)
    for slot in range(len(slab_refs)):
        part = jnp.exp(exp_ref[:, slot * step : (slot + 1) * step] - top)
        exp_ref[:, slot * step : (slot + 1) * step] = part
        total += jnp.sum(part, axis=-1, keepdims=True)
    stat_ref[:, :LANES] = jnp.broadcast_to(top, (q.shape[0], LANES))
    stat_ref[:, LANES : 2 * LANES] = jnp.broadcast_to(total, (q.shape[0], LANES))
    stat_ref[:, 2 * LANES :] = q.astype(jnp.float32)


def split(grad):
    hi = grad.astype(jnp.bfloat16)
    return hi, (grad - hi.astype(jnp.float32)).astype(jnp.bfloat16)


def named_kernel(named_ref, stat_ref, hi_ref, lo_ref, named_out, share_ref, keys_ref, l_ref):
    width = keys_ref.shape[1]
    col_tiles = width // LANES
    row_tiles = named_ref.shape[0] // col_tiles
    piece_rows = named_ref.shape[1]
    named_rows = row_tiles * piece_rows
    scaling = 4.0 / math.sqrt(width)
    join_pieces(named_ref, keys_ref, row_tiles, col_tiles)
    q = stat_ref[:, 2 * LANES :].astype(jnp.bfloat16)
    pool_top = stat_ref[:, :1]
    top = pool_top
    for c in range(0, named_rows, STEP):
        part = dot_nt(q, keys_ref[c : c + STEP, :]) * scaling
        l_ref[:, c : c + STEP] = part
        top = jnp.maximum(top, jnp.max(part, axis=-1, keepdims=True))
    pool_scale = jnp.exp(pool_top - top)
    total = stat_ref[:, LANES : LANES + 1] * pool_scale
    for c in range(0, named_rows, STEP):
        part = jnp.exp(l_ref[:, c : c + STEP] - top)
        l_ref[:, c : c + STEP] = part
        total += jnp.sum(part, axis=-1, keepdims=True)
    share = 1.0 / total
    share_ref[...] = jnp.broadcast_to(share * pool_scale, share_ref.shape)
    for c in range(0, named_rows, STEP):
        hi, lo = split(l_ref[:, c : c + STEP] * share)
        hi_ref[:, c : c + STEP] = hi
        lo_ref[:, c : c + STEP] = lo
        terms = (dot_tn(hi, q) + dot_tn(lo, q)) * (scaling * LIFT)
        first = c // piece_rows
        for r in range(STEP // piece_rows):
            for k in range(col_tiles):
                named_out[(first + r) * col_tiles + k] = terms[
                    r * piece_rows : (r + 1) * piece_rows, k * LANES : (k + 1) * LANES
                ]


def pool_grad_kernel(place_ref, q_ref, exp_ref, share_ref, pos_ref, hi_ref, lo_ref, *grad_refs):
    queries, width = q_ref.shape
    step = grad_refs[0].shape[0]
    scaling = 4.0 / math.sqrt(width)
    q = q_ref[...]
    share = share_ref[:, :1]
    across = lax.broadcasted_iota(jnp.int32, (queries, queries), 1)
    down = lax.broadcasted_iota(jnp.int32, (queries, queries), 0)
    pos = jnp.sum(jnp.where(across == down, pos_ref[...].astype(jnp.float32), 0.0), axis=1, keepdims=True)
    pos = pos.astype(jnp.int32)
    block = step // place_ref.shape[0]
    for slot, grad_ref in enumerate(grad_refs):
        first, last = slot * step, (slot + 1) * step
        columns = lax.broadcasted_iota(jnp.int32, (queries, step), 1) + first
        hi, lo = split(exp_ref[:, first:last] * share - (columns == pos).astype(jnp.float32))
        hi_ref[:, first:last] = hi
        lo_ref[:, first:last] = lo
        terms = (dot_tn(hi, q) + dot_tn(lo, q)) * (scaling * LIFT)
        for r in range(step // block):
            grad_ref[pl.ds(pl.multiple_of(place_ref[r] * block, block), block), :] = terms[r * block : (r + 1) * block]


def query_kernel(pool_hi_ref, pool_lo_ref, hi_ref, lo_ref, named_ref, *refs):
    slab_refs, out_ref, keys_ref = refs[:-2], refs[-2], refs[-1]
    step, width = slab_refs[0].shape
    col_tiles = width // LANES
    row_tiles = named_ref.shape[0] // col_tiles
    scaling = 4.0 / math.sqrt(width)
    join_pieces(named_ref, keys_ref, row_tiles, col_tiles)
    total = dot_nn(hi_ref[...], keys_ref[...]) + dot_nn(lo_ref[...], keys_ref[...])
    for slot, slab_ref in enumerate(slab_refs):
        first, last = slot * step, (slot + 1) * step
        total += dot_nn(pool_hi_ref[:, first:last], slab_ref[...])
        total += dot_nn(pool_lo_ref[:, first:last], slab_ref[...])
    out_ref[...] = total * scaling


def call(kernel, outs, scratch, flops, *args, smem=0, after=()):
    vmem = pl.BlockSpec(memory_space=pltpu.VMEM)
    specs = [pl.BlockSpec(memory_space=pltpu.SMEM)] * smem + [vmem] * (len(args) - smem)
    specs += [pl.BlockSpec(memory_space=pltpu.HBM)] * len(after)
    count = len(args)

    def body(*refs):
        kernel(*refs[:count], *refs[count + len(after) :])

    return pl.pallas_call(
        body,
        out_shape=tuple(jax.ShapeDtypeStruct(shape, dtype) for shape, dtype in outs),
        in_specs=specs,
        out_specs=(vmem,) * len(outs),
        scratch_shapes=scratch,
        compiler_params=pltpu.CompilerParams(vmem_limit_bytes=VMEM),
        cost_estimate=pl.CostEstimate(flops=flops, bytes_accessed=4 * 1024 * 1024, transcendentals=0),
    )(*args, *after)


def local(queries, passages, positive, negative_owners):
    query_count, width = queries.shape
    block_rows = passages.shape[0]
    neg_count = negative_owners.shape[1]
    f32, bf16, half = jnp.float32, jnp.bfloat16, jnp.float16
    wide, members, runs = lax.axis_size(WIDE), lax.axis_size(RUN), lax.axis_size("zs")
    near, far = lax.axis_size("yh"), lax.axis_size("x")
    row_tiles, col_tiles = block_rows // SUBS, width // LANES
    tiles = row_tiles * col_tiles // members
    pool_rows = far * near * block_rows
    named_rows = neg_count * block_rows
    swaps = [[(i, i ^ k) for i in range(near)] for k in range(near)]
    here_x, here_y = lax.axis_index("x"), lax.axis_index("yh")
    run = lax.axis_index("zs").astype(jnp.int32)[None]

    pieces = passages.reshape(row_tiles, SUBS, col_tiles, LANES).transpose(0, 2, 1, 3)
    pieces = pieces.reshape(members, tiles * SUBS, LANES)
    names = jnp.pad(negative_owners[0].astype(bf16), (0, LANES - neg_count))
    rows = tiles * SUBS
    shape = (runs, members, rows + SUBS, LANES)
    row = lax.broadcasted_iota(jnp.int32, shape, 2)
    sent = jnp.pad(pieces, ((0, 0), (0, SUBS), (0, 0)))
    sent = jnp.where(row < rows, jnp.broadcast_to(sent[None], shape), jnp.broadcast_to(names, shape))
    sent = sent.reshape(wide, rows + SUBS, LANES)
    with jax.named_scope("spread_pieces"):
        spread = lax.all_to_all(sent, WIDE, 0, 0, tiled=True)
    owners = spread[:, tiles * SUBS, :neg_count].astype(jnp.int32).reshape(wide * neg_count)

    with jax.named_scope("pool_yh"):
        mine = lax.all_gather(passages, "yh", axis=0, tiled=True)
    with jax.named_scope("pool_x"):
        slabs = [mine] + [lax.ppermute(mine, "x", swaps[k]) for k in range(1, far)]
    slots = positive ^ (here_x * (near * block_rows))

    (picked,) = call(
        pick_kernel,
        [((members, tiles, neg_count, SUBS, LANES), bf16)],
        [],
        0,
        run,
        owners,
        spread.reshape(wide * (tiles + 1), SUBS, LANES),
        smem=2,
        after=(mine,),
    )
    with jax.named_scope("named_pieces"):
        named = lax.all_to_all(picked, RUN, 0, 0, tiled=True)
    named = named.reshape(members * tiles, neg_count * SUBS, LANES)

    product = 2 * query_count * width
    exps, stats = call(
        pool_kernel,
        [((query_count, pool_rows), f32), ((query_count, 2 * LANES + width), f32)],
        [],
        100 * product * pool_rows,
        queries,
        *slabs,
    )
    named_hi, named_lo, named_grad, share = call(
        named_kernel,
        [
            ((query_count, named_rows), bf16),
            ((query_count, named_rows), bf16),
            ((members * tiles, neg_count * SUBS, LANES), f32),
            ((query_count, LANES), f32),
        ],
        [pltpu.VMEM((named_rows, width), bf16), pltpu.VMEM((query_count, named_rows), f32)],
        3 * product * named_rows,
        named,
        stats,
    )
    with jax.named_scope("named_back"):
        back = named_grad.astype(half).reshape(members, tiles, neg_count, SUBS, LANES)
        back = lax.all_to_all(back, RUN, 0, 0, tiled=True)

    pool_hi, pool_lo, *pool_grads = call(
        pool_grad_kernel,
        [((query_count, pool_rows), bf16)] * 2 + [((near * block_rows, width), f32)] * far,
        [],
        2 * product * pool_rows,
        jnp.arange(near, dtype=jnp.int32) ^ here_y.astype(jnp.int32),
        queries,
        exps,
        share,
        slots[None, :],
        smem=1,
    )
    rows_x = pool_grads[0]
    leaving = [grad.astype(half) for grad in pool_grads[1:]]
    with jax.named_scope("grad_x"):
        for k in range(1, far):
            part = lax.ppermute(leaving[k - 1], "x", swaps[k])
            rows_x = rows_x + part.astype(f32)
    owned = rows_x[:block_rows]
    with jax.named_scope("grad_yh"):
        for k in (2, 1, 3):
            part = (rows_x[k * block_rows : (k + 1) * block_rows] * (1.0 / far)).astype(half)
            part = lax.ppermute(part, "yh", swaps[k])
            owned = owned + part.astype(f32) * float(far)

    (query_grad,) = call(
        query_kernel,
        [((query_count, width), f32)],
        [pltpu.VMEM((named_rows, width), bf16)],
        8 * product * (pool_rows + named_rows),
        pool_hi,
        pool_lo,
        named_hi,
        named_lo,
        named,
        *slabs,
        after=(rows_x,),
    )

    (summed,) = call(
        gather_sum_kernel,
        [((wide, tiles, SUBS, LANES), f32)],
        [pltpu.VMEM((wide, SUBS, LANES), f32)] * tiles,
        0,
        run,
        owners,
        back.astype(f32),
        smem=2,
    )
    with jax.named_scope("pieces_home"):
        home = lax.all_to_all(summed.astype(half), WIDE, 0, 0, tiled=True)
    home = home.astype(f32).reshape(runs, row_tiles, col_tiles, SUBS, LANES)
    returned = home.sum(0).transpose(0, 2, 1, 3).reshape(block_rows, width)
    return (query_grad, owned * (1.0 / LIFT) + returned * (1.0 / (LIFT * DROP)))


def solution(mesh):
    whole = Mesh(mesh.devices.reshape(4, 3, 2, 2, 4, 4), AXES)
    spec = P(AXES, None)
    return jax.shard_map(
        local,
        mesh=whole,
        in_specs=(spec, spec, P(AXES), spec),
        out_specs=(spec, spec),
        check_vma=False,
    )
```

```python
import functools
import math

import jax
import jax.numpy as jnp
from jax import lax
from jax.experimental import pallas as pl
from jax.experimental.pallas import tpu as pltpu
from jax.sharding import Mesh
from jax.sharding import PartitionSpec as P

AXES = ("zs", "zl", "yl", "c", "x", "yh")
WIDE = ("zs", "zl", "yl", "c")
RUN = ("zl", "yl", "c")
LANES = 128
SUBS = 8
LIFT = 128.0
DROP = 1.0 / 16.0
VMEM = 16 * 1024 * 1024
STEP = 256


def dot_nt(a, b):
    return lax.dot_general(a, b, (((1,), (1,)), ((), ())), preferred_element_type=jnp.float32)


def dot_tn(a, b):
    return lax.dot_general(a, b, (((0,), (0,)), ((), ())), preferred_element_type=jnp.float32)


def dot_nn(a, b):
    return lax.dot_general(a, b, (((1,), (0,)), ((), ())), preferred_element_type=jnp.float32)


def join_pieces(named_ref, keys_ref, row_tiles, col_tiles):
    rows = named_ref.shape[1]
    for r in range(row_tiles):
        for c in range(col_tiles):
            keys_ref[r * rows : (r + 1) * rows, c * LANES : (c + 1) * LANES] = named_ref[r * col_tiles + c]


def pick_kernel(run_ref, owners_ref, held_ref, out_ref):
    members, tiles, count = out_ref.shape[:3]
    stride = held_ref.shape[0] // (owners_ref.shape[0] // count)

    first = run_ref[0] * members
    for i in range(members):
        for k in range(count):
            owner = owners_ref[(first + i) * count + k]
            for u in range(tiles):
                out_ref[i, u, k] = held_ref[owner * stride + u]


def gather_sum_kernel(run_ref, owners_ref, terms_ref, out_ref, *acc_refs):
    members, tiles, count = terms_ref.shape[:3]
    for u in range(tiles):
        acc_refs[u][...] = jnp.zeros_like(acc_refs[u])

    def body(i, carry):
        for k in range(count):
            owner = owners_ref[(run_ref[0] * members + i) * count + k]
            for u in range(tiles):
                acc_refs[u][owner] += terms_ref[i, u, k]
        return carry

    lax.fori_loop(0, members, body, 0)
    for u in range(tiles):
        out_ref[:, u] = acc_refs[u][...] * DROP


def pool_kernel(q_ref, *refs):
    slab_refs, (exp_ref, stat_ref) = refs[:-2], refs[-2:]
    width = q_ref.shape[1]
    step = slab_refs[0].shape[0]
    scaling = 4.0 / math.sqrt(width)
    q = q_ref[...]
    top = None
    for slot, slab_ref in enumerate(slab_refs):
        part = dot_nt(q, slab_ref[...]) * scaling
        exp_ref[:, slot * step : (slot + 1) * step] = part
        high = jnp.max(part, axis=-1, keepdims=True)
        top = high if top is None else jnp.maximum(top, high)
    total = jnp.zeros_like(top)
    for slot in range(len(slab_refs)):
        part = jnp.exp(exp_ref[:, slot * step : (slot + 1) * step] - top)
        exp_ref[:, slot * step : (slot + 1) * step] = part
        total += jnp.sum(part, axis=-1, keepdims=True)
    stat_ref[:, :LANES] = jnp.broadcast_to(top, (q.shape[0], LANES))
    stat_ref[:, LANES : 2 * LANES] = jnp.broadcast_to(total, (q.shape[0], LANES))
    stat_ref[:, 2 * LANES :] = q.astype(jnp.float32)


def split(grad):
    hi = grad.astype(jnp.bfloat16)
    return hi, (grad - hi.astype(jnp.float32)).astype(jnp.bfloat16)


def named_kernel(named_ref, stat_ref, hi_ref, lo_ref, named_out, share_ref, keys_ref, l_ref):
    width = keys_ref.shape[1]
    col_tiles = width // LANES
    row_tiles = named_ref.shape[0] // col_tiles
    piece_rows = named_ref.shape[1]
    named_rows = row_tiles * piece_rows
    scaling = 4.0 / math.sqrt(width)
    join_pieces(named_ref, keys_ref, row_tiles, col_tiles)
    q = stat_ref[:, 2 * LANES :].astype(jnp.bfloat16)
    pool_top = stat_ref[:, :1]
    top = pool_top
    for c in range(0, named_rows, STEP):
        part = dot_nt(q, keys_ref[c : c + STEP, :]) * scaling
        l_ref[:, c : c + STEP] = part
        top = jnp.maximum(top, jnp.max(part, axis=-1, keepdims=True))
    pool_scale = jnp.exp(pool_top - top)
    total = stat_ref[:, LANES : LANES + 1] * pool_scale
    for c in range(0, named_rows, STEP):
        part = jnp.exp(l_ref[:, c : c + STEP] - top)
        l_ref[:, c : c + STEP] = part
        total += jnp.sum(part, axis=-1, keepdims=True)
    share = 1.0 / total
    share_ref[...] = jnp.broadcast_to(share * pool_scale, share_ref.shape)
    for c in range(0, named_rows, STEP):
        hi, lo = split(l_ref[:, c : c + STEP] * share)
        hi_ref[:, c : c + STEP] = hi
        lo_ref[:, c : c + STEP] = lo
        terms = (dot_tn(hi, q) + dot_tn(lo, q)) * (scaling * LIFT)
        first = c // piece_rows
        for r in range(STEP // piece_rows):
            for k in range(col_tiles):
                named_out[(first + r) * col_tiles + k] = terms[
                    r * piece_rows : (r + 1) * piece_rows, k * LANES : (k + 1) * LANES
                ]


def pool_grad_kernel(place_ref, q_ref, exp_ref, share_ref, pos_ref, hi_ref, lo_ref, *grad_refs):
    queries, width = q_ref.shape
    step = grad_refs[0].shape[0]
    scaling = 4.0 / math.sqrt(width)
    q = q_ref[...]
    share = share_ref[:, :1]
    across = lax.broadcasted_iota(jnp.int32, (queries, queries), 1)
    down = lax.broadcasted_iota(jnp.int32, (queries, queries), 0)
    pos = jnp.sum(jnp.where(across == down, pos_ref[...].astype(jnp.float32), 0.0), axis=1, keepdims=True)
    pos = pos.astype(jnp.int32)
    block = step // place_ref.shape[0]
    for slot, grad_ref in enumerate(grad_refs):
        first, last = slot * step, (slot + 1) * step
        columns = lax.broadcasted_iota(jnp.int32, (queries, step), 1) + first
        hi, lo = split(exp_ref[:, first:last] * share - (columns == pos).astype(jnp.float32))
        hi_ref[:, first:last] = hi
        lo_ref[:, first:last] = lo
        terms = (dot_tn(hi, q) + dot_tn(lo, q)) * (scaling * LIFT)
        for r in range(step // block):
            grad_ref[pl.ds(pl.multiple_of(place_ref[r] * block, block), block), :] = terms[r * block : (r + 1) * block]


def query_kernel(pool_hi_ref, pool_lo_ref, hi_ref, lo_ref, named_ref, *refs):
    slab_refs, out_ref, keys_ref = refs[:-2], refs[-2], refs[-1]
    step, width = slab_refs[0].shape
    col_tiles = width // LANES
    row_tiles = named_ref.shape[0] // col_tiles
    scaling = 4.0 / math.sqrt(width)
    join_pieces(named_ref, keys_ref, row_tiles, col_tiles)
    total = dot_nn(hi_ref[...], keys_ref[...]) + dot_nn(lo_ref[...], keys_ref[...])
    for slot, slab_ref in enumerate(slab_refs):
        first, last = slot * step, (slot + 1) * step
        total += dot_nn(pool_hi_ref[:, first:last], slab_ref[...])
        total += dot_nn(pool_lo_ref[:, first:last], slab_ref[...])
    out_ref[...] = total * scaling


def call(kernel, outs, scratch, flops, *args, smem=0, after=()):
    vmem = pl.BlockSpec(memory_space=pltpu.VMEM)
    specs = [pl.BlockSpec(memory_space=pltpu.SMEM)] * smem + [vmem] * (len(args) - smem)
    specs += [pl.BlockSpec(memory_space=pltpu.HBM)] * len(after)
    count = len(args)

    def body(*refs):
        kernel(*refs[:count], *refs[count + len(after) :])

    return pl.pallas_call(
        body,
        out_shape=tuple(jax.ShapeDtypeStruct(shape, dtype) for shape, dtype in outs),
        in_specs=specs,
        out_specs=(vmem,) * len(outs),
        scratch_shapes=scratch,
        compiler_params=pltpu.CompilerParams(vmem_limit_bytes=VMEM),
        cost_estimate=pl.CostEstimate(flops=flops, bytes_accessed=4 * 1024 * 1024, transcendentals=0),
    )(*args, *after)


def local(queries, passages, positive, negative_owners):
    query_count, width = queries.shape
    block_rows = passages.shape[0]
    neg_count = negative_owners.shape[1]
    f32, bf16, half = jnp.float32, jnp.bfloat16, jnp.float16
    wide, members, runs = lax.axis_size(WIDE), lax.axis_size(RUN), lax.axis_size("zs")
    near, far = lax.axis_size("yh"), lax.axis_size("x")
    row_tiles, col_tiles = block_rows // SUBS, width // LANES
    tiles = row_tiles * col_tiles // members
    pool_rows = far * near * block_rows
    named_rows = neg_count * block_rows
    swaps = [[(i, i ^ k) for i in range(near)] for k in range(near)]
    here_x, here_y = lax.axis_index("x"), lax.axis_index("yh")
    run = lax.axis_index("zs").astype(jnp.int32)[None]

    pieces = passages.reshape(row_tiles, SUBS, col_tiles, LANES).transpose(0, 2, 1, 3)
    pieces = pieces.reshape(members, tiles * SUBS, LANES)
    names = jnp.pad(negative_owners[0].astype(bf16), (0, LANES - neg_count))
    rows = tiles * SUBS
    shape = (runs, members, rows + SUBS, LANES)
    row = lax.broadcasted_iota(jnp.int32, shape, 2)
    sent = jnp.pad(pieces, ((0, 0), (0, SUBS), (0, 0)))
    sent = jnp.where(row < rows, jnp.broadcast_to(sent[None], shape), jnp.broadcast_to(names, shape))
    sent = sent.reshape(wide, rows + SUBS, LANES)
    with jax.named_scope("spread_pieces"):
        spread = lax.all_to_all(sent, WIDE, 0, 0, tiled=True)
    owners = spread[:, tiles * SUBS, :neg_count].astype(jnp.int32).reshape(wide * neg_count)

    with jax.named_scope("pool_yh"):
        mine = lax.all_gather(passages, "yh", axis=0, tiled=True)
    with jax.named_scope("pool_x"):
        slabs = [mine] + [lax.ppermute(mine, "x", swaps[k]) for k in range(1, far)]
    slots = positive ^ (here_x * (near * block_rows))

    (picked,) = call(
        pick_kernel,
        [((members, tiles, neg_count, SUBS, LANES), bf16)],
        [],
        0,
        run,
        owners,
        spread.reshape(wide * (tiles + 1), SUBS, LANES),
        smem=2,
        after=(mine,),
    )
    with jax.named_scope("named_pieces"):
        named = lax.all_to_all(picked, RUN, 0, 0, tiled=True)
    named = named.reshape(members * tiles, neg_count * SUBS, LANES)

    product = 2 * query_count * width
    exps, stats = call(
        pool_kernel,
        [((query_count, pool_rows), f32), ((query_count, 2 * LANES + width), f32)],
        [],
        100 * product * pool_rows,
        queries,
        *slabs,
    )
    named_hi, named_lo, named_grad, share = call(
        named_kernel,
        [
            ((query_count, named_rows), bf16),
            ((query_count, named_rows), bf16),
            ((members * tiles, neg_count * SUBS, LANES), f32),
            ((query_count, LANES), f32),
        ],
        [pltpu.VMEM((named_rows, width), bf16), pltpu.VMEM((query_count, named_rows), f32)],
        3 * product * named_rows,
        named,
        stats,
    )
    with jax.named_scope("named_back"):
        back = named_grad.astype(half).reshape(members, tiles, neg_count, SUBS, LANES)
        back = lax.all_to_all(back, RUN, 0, 0, tiled=True)

    pool_hi, pool_lo, *pool_grads = call(
        pool_grad_kernel,
        [((query_count, pool_rows), bf16)] * 2 + [((near * block_rows, width), f32)] * far,
        [],
        2 * product * pool_rows,
        jnp.arange(near, dtype=jnp.int32) ^ here_y.astype(jnp.int32),
        queries,
        exps,
        share,
        slots[None, :],
        smem=1,
    )
    rows_x = pool_grads[0]
    leaving = [grad.astype(half) for grad in pool_grads[1:]]
    with jax.named_scope("grad_x"):
        for k in range(1, far):
            part = lax.ppermute(leaving[k - 1], "x", swaps[k])
            rows_x = rows_x + part.astype(f32)
    owned = rows_x[:block_rows]
    with jax.named_scope("grad_yh"):
        for k in (2, 1, 3):
            part = (rows_x[k * block_rows : (k + 1) * block_rows] * (1.0 / far)).astype(half)
            part = lax.ppermute(part, "yh", swaps[k])
            owned = owned + part.astype(f32) * float(far)

    (query_grad,) = call(
        query_kernel,
        [((query_count, width), f32)],
        [pltpu.VMEM((named_rows, width), bf16)],
        8 * product * (pool_rows + named_rows),
        pool_hi,
        pool_lo,
        named_hi,
        named_lo,
        named,
        *slabs,
        after=(rows_x,),
    )

    (summed,) = call(
        gather_sum_kernel,
        [((wide, tiles, SUBS, LANES), f32)],
        [pltpu.VMEM((wide, SUBS, LANES), f32)] * tiles,
        0,
        run,
        owners,
        back.astype(f32),
        smem=2,
    )
    with jax.named_scope("pieces_home"):
        home = lax.all_to_all(summed.astype(half), WIDE, 0, 0, tiled=True)
    home = home.reshape(runs, row_tiles, col_tiles, SUBS, LANES).transpose(0, 1, 3, 2, 4)
    home = home.reshape(runs * block_rows, width)
    returned = home[:block_rows].astype(f32)
    for r in range(1, runs):
        returned = returned + home[r * block_rows : (r + 1) * block_rows].astype(f32)
    return (query_grad, owned * (1.0 / LIFT) + returned * (1.0 / (LIFT * DROP)))


def solution(mesh):
    whole = Mesh(mesh.devices.reshape(4, 3, 2, 2, 4, 4), AXES)
    spec = P(AXES, None)
    return jax.shard_map(
        local,
        mesh=whole,
        in_specs=(spec, spec, P(AXES), spec),
        out_specs=(spec, spec),
        check_vma=False,
    )
```

```python
import functools
import math

import jax
import jax.numpy as jnp
from jax import lax
from jax.experimental import pallas as pl
from jax.experimental.pallas import tpu as pltpu
from jax.sharding import Mesh
from jax.sharding import PartitionSpec as P

AXES = ("zs", "zl", "yl", "c", "x", "yh")
WIDE = ("zs", "zl", "yl", "c")
RUN = ("zl", "yl", "c")
LANES = 128
SUBS = 8
LIFT = 128.0
DROP = 1.0 / 16.0
VMEM = 16 * 1024 * 1024
STEP = 256


def dot_nt(a, b):
    return lax.dot_general(a, b, (((1,), (1,)), ((), ())), preferred_element_type=jnp.float32)


def dot_tn(a, b):
    return lax.dot_general(a, b, (((0,), (0,)), ((), ())), preferred_element_type=jnp.float32)


def dot_nn(a, b):
    return lax.dot_general(a, b, (((1,), (0,)), ((), ())), preferred_element_type=jnp.float32)


def join_pieces(named_ref, keys_ref, row_tiles, col_tiles):
    rows = named_ref.shape[1]
    for r in range(row_tiles):
        for c in range(col_tiles):
            keys_ref[r * rows : (r + 1) * rows, c * LANES : (c + 1) * LANES] = named_ref[r * col_tiles + c]


def pick_kernel(run_ref, owners_ref, held_ref, out_ref):
    members, tiles, count = out_ref.shape[:3]
    stride = held_ref.shape[0] // (owners_ref.shape[0] // count)

    first = run_ref[0] * members
    for i in range(members):
        for k in range(count):
            owner = owners_ref[(first + i) * count + k]
            for u in range(tiles):
                out_ref[i, u, k] = held_ref[owner * stride + u]


def gather_sum_kernel(run_ref, owners_ref, terms_ref, out_ref, *acc_refs):
    members, tiles, count = terms_ref.shape[:3]
    for u in range(tiles):
        acc_refs[u][...] = jnp.zeros_like(acc_refs[u])

    def body(i, carry):
        for k in range(count):
            owner = owners_ref[(run_ref[0] * members + i) * count + k]
            for u in range(tiles):
                acc_refs[u][owner] += terms_ref[i, u, k]
        return carry

    lax.fori_loop(0, members, body, 0)
    for u in range(tiles):
        out_ref[:, u] = acc_refs[u][...] * DROP


def pool_kernel(q_ref, *refs):
    slab_refs, (exp_ref, stat_ref) = refs[:-2], refs[-2:]
    width = q_ref.shape[1]
    step = slab_refs[0].shape[0]
    scaling = 4.0 / math.sqrt(width)
    q = q_ref[...]
    top = None
    for slot, slab_ref in enumerate(slab_refs):
        part = dot_nt(q, slab_ref[...]) * scaling
        exp_ref[:, slot * step : (slot + 1) * step] = part
        high = jnp.max(part, axis=-1, keepdims=True)
        top = high if top is None else jnp.maximum(top, high)
    total = jnp.zeros_like(top)
    for slot in range(len(slab_refs)):
        part = jnp.exp(exp_ref[:, slot * step : (slot + 1) * step] - top)
        exp_ref[:, slot * step : (slot + 1) * step] = part
        total += jnp.sum(part, axis=-1, keepdims=True)
    stat_ref[:, :LANES] = jnp.broadcast_to(top, (q.shape[0], LANES))
    stat_ref[:, LANES : 2 * LANES] = jnp.broadcast_to(total, (q.shape[0], LANES))
    stat_ref[:, 2 * LANES :] = q.astype(jnp.float32)


def split(grad):
    hi = grad.astype(jnp.bfloat16)
    return hi, (grad - hi.astype(jnp.float32)).astype(jnp.bfloat16)


def named_kernel(named_ref, stat_ref, hi_ref, lo_ref, named_out, share_ref, keys_ref, l_ref):
    width = keys_ref.shape[1]
    col_tiles = width // LANES
    row_tiles = named_ref.shape[0] // col_tiles
    piece_rows = named_ref.shape[1]
    named_rows = row_tiles * piece_rows
    scaling = 4.0 / math.sqrt(width)
    join_pieces(named_ref, keys_ref, row_tiles, col_tiles)
    q = stat_ref[:, 2 * LANES :].astype(jnp.bfloat16)
    pool_top = stat_ref[:, :1]
    top = pool_top
    for c in range(0, named_rows, STEP):
        part = dot_nt(q, keys_ref[c : c + STEP, :]) * scaling
        l_ref[:, c : c + STEP] = part
        top = jnp.maximum(top, jnp.max(part, axis=-1, keepdims=True))
    pool_scale = jnp.exp(pool_top - top)
    total = stat_ref[:, LANES : LANES + 1] * pool_scale
    for c in range(0, named_rows, STEP):
        part = jnp.exp(l_ref[:, c : c + STEP] - top)
        l_ref[:, c : c + STEP] = part
        total += jnp.sum(part, axis=-1, keepdims=True)
    share = 1.0 / total
    share_ref[...] = jnp.broadcast_to(share * pool_scale, share_ref.shape)
    for c in range(0, named_rows, STEP):
        hi, lo = split(l_ref[:, c : c + STEP] * share)
        hi_ref[:, c : c + STEP] = hi
        lo_ref[:, c : c + STEP] = lo
        terms = (dot_tn(hi, q) + dot_tn(lo, q)) * (scaling * LIFT)
        first = c // piece_rows
        for r in range(STEP // piece_rows):
            for k in range(col_tiles):
                named_out[(first + r) * col_tiles + k] = terms[
                    r * piece_rows : (r + 1) * piece_rows, k * LANES : (k + 1) * LANES
                ]


def pool_grad_kernel(place_ref, q_ref, exp_ref, share_ref, pos_ref, hi_ref, lo_ref, *grad_refs):
    queries, width = q_ref.shape
    step = grad_refs[0].shape[0]
    scaling = 4.0 / math.sqrt(width)
    q = q_ref[...]
    share = share_ref[:, :1]
    across = lax.broadcasted_iota(jnp.int32, (queries, queries), 1)
    down = lax.broadcasted_iota(jnp.int32, (queries, queries), 0)
    pos = jnp.sum(jnp.where(across == down, pos_ref[...].astype(jnp.float32), 0.0), axis=1, keepdims=True)
    pos = pos.astype(jnp.int32)
    block = step // place_ref.shape[0]
    for slot, grad_ref in enumerate(grad_refs):
        first, last = slot * step, (slot + 1) * step
        columns = lax.broadcasted_iota(jnp.int32, (queries, step), 1) + first
        hi, lo = split(exp_ref[:, first:last] * share - (columns == pos).astype(jnp.float32))
        hi_ref[:, first:last] = hi
        lo_ref[:, first:last] = lo
        terms = (dot_tn(hi, q) + dot_tn(lo, q)) * (scaling * LIFT)
        for r in range(step // block):
            grad_ref[pl.ds(pl.multiple_of(place_ref[r] * block, block), block), :] = terms[r * block : (r + 1) * block]


def query_kernel(pool_hi_ref, pool_lo_ref, hi_ref, lo_ref, named_ref, *refs):
    slab_refs, out_ref, keys_ref = refs[:-2], refs[-2], refs[-1]
    step, width = slab_refs[0].shape
    col_tiles = width // LANES
    row_tiles = named_ref.shape[0] // col_tiles
    scaling = 4.0 / math.sqrt(width)
    join_pieces(named_ref, keys_ref, row_tiles, col_tiles)
    total = dot_nn(hi_ref[...], keys_ref[...]) + dot_nn(lo_ref[...], keys_ref[...])
    for slot, slab_ref in enumerate(slab_refs):
        first, last = slot * step, (slot + 1) * step
        total += dot_nn(pool_hi_ref[:, first:last], slab_ref[...])
        total += dot_nn(pool_lo_ref[:, first:last], slab_ref[...])
    out_ref[...] = total * scaling


def call(kernel, outs, scratch, flops, *args, smem=0, after=()):
    vmem = pl.BlockSpec(memory_space=pltpu.VMEM)
    specs = [pl.BlockSpec(memory_space=pltpu.SMEM)] * smem + [vmem] * (len(args) - smem)
    specs += [pl.BlockSpec(memory_space=pltpu.HBM)] * len(after)
    count = len(args)

    def body(*refs):
        kernel(*refs[:count], *refs[count + len(after) :])

    return pl.pallas_call(
        body,
        out_shape=tuple(jax.ShapeDtypeStruct(shape, dtype) for shape, dtype in outs),
        in_specs=specs,
        out_specs=(vmem,) * len(outs),
        scratch_shapes=scratch,
        compiler_params=pltpu.CompilerParams(vmem_limit_bytes=VMEM),
        cost_estimate=pl.CostEstimate(flops=flops, bytes_accessed=4 * 1024 * 1024, transcendentals=0),
    )(*args, *after)


def local(queries, passages, positive, negative_owners):
    query_count, width = queries.shape
    block_rows = passages.shape[0]
    neg_count = negative_owners.shape[1]
    f32, bf16, half = jnp.float32, jnp.bfloat16, jnp.float16
    wide, members, runs = lax.axis_size(WIDE), lax.axis_size(RUN), lax.axis_size("zs")
    near, far = lax.axis_size("yh"), lax.axis_size("x")
    row_tiles, col_tiles = block_rows // SUBS, width // LANES
    tiles = row_tiles * col_tiles // members
    pool_rows = far * near * block_rows
    named_rows = neg_count * block_rows
    swaps = [[(i, i ^ k) for i in range(near)] for k in range(near)]
    here_x, here_y = lax.axis_index("x"), lax.axis_index("yh")
    run = lax.axis_index("zs").astype(jnp.int32)[None]

    pieces = passages.reshape(row_tiles, SUBS, col_tiles, LANES).transpose(0, 2, 1, 3)
    pieces = pieces.reshape(members, tiles * SUBS, LANES)
    rows = tiles * SUBS
    names = jnp.pad(negative_owners, ((0, SUBS - 1), (0, LANES - neg_count))).astype(bf16)
    names = jnp.pad(names, ((rows, 0), (0, 0)))
    shape = (runs, members, rows + SUBS, LANES)
    row = lax.broadcasted_iota(jnp.int32, shape, 2)
    sent = jnp.pad(pieces, ((0, 0), (0, SUBS), (0, 0)))
    sent = jnp.where(row < rows, jnp.broadcast_to(sent[None], shape), jnp.broadcast_to(names[None, None], shape))
    sent = sent.reshape(wide, rows + SUBS, LANES)
    with jax.named_scope("spread_pieces"):
        spread = lax.all_to_all(sent, WIDE, 0, 0, tiled=True)
    owners = spread[:, tiles * SUBS, :neg_count].astype(jnp.int32).reshape(wide * neg_count)

    with jax.named_scope("pool_yh"):
        mine = lax.all_gather(passages, "yh", axis=0, tiled=True)
    with jax.named_scope("pool_x"):
        slabs = [mine] + [lax.ppermute(mine, "x", swaps[k]) for k in range(1, far)]
    slots = positive ^ (here_x * (near * block_rows))

    (picked,) = call(
        pick_kernel,
        [((members, tiles, neg_count, SUBS, LANES), bf16)],
        [],
        0,
        run,
        owners,
        spread.reshape(wide * (tiles + 1), SUBS, LANES),
        smem=2,
        after=(mine,),
    )
    with jax.named_scope("named_pieces"):
        named = lax.all_to_all(picked, RUN, 0, 0, tiled=True)
    named = named.reshape(members * tiles, neg_count * SUBS, LANES)

    product = 2 * query_count * width
    exps, stats = call(
        pool_kernel,
        [((query_count, pool_rows), f32), ((query_count, 2 * LANES + width), f32)],
        [],
        100 * product * pool_rows,
        queries,
        *slabs,
    )
    named_hi, named_lo, named_grad, share = call(
        named_kernel,
        [
            ((query_count, named_rows), bf16),
            ((query_count, named_rows), bf16),
            ((members * tiles, neg_count * SUBS, LANES), f32),
            ((query_count, LANES), f32),
        ],
        [pltpu.VMEM((named_rows, width), bf16), pltpu.VMEM((query_count, named_rows), f32)],
        3 * product * named_rows,
        named,
        stats,
    )
    with jax.named_scope("named_back"):
        back = named_grad.astype(half).reshape(members, tiles, neg_count, SUBS, LANES)
        back = lax.all_to_all(back, RUN, 0, 0, tiled=True)

    pool_hi, pool_lo, *pool_grads = call(
        pool_grad_kernel,
        [((query_count, pool_rows), bf16)] * 2 + [((near * block_rows, width), f32)] * far,
        [],
        2 * product * pool_rows,
        jnp.arange(near, dtype=jnp.int32) ^ here_y.astype(jnp.int32),
        queries,
        exps,
        share,
        slots[None, :],
        smem=1,
    )
    rows_x = pool_grads[0]
    leaving = [grad.astype(half) for grad in pool_grads[1:]]
    with jax.named_scope("grad_x"):
        for k in range(1, far):
            part = lax.ppermute(leaving[k - 1], "x", swaps[k])
            rows_x = rows_x + part.astype(f32)
    owned = rows_x[:block_rows]
    with jax.named_scope("grad_yh"):
        for k in (2, 1, 3):
            part = (rows_x[k * block_rows : (k + 1) * block_rows] * (1.0 / far)).astype(half)
            part = lax.ppermute(part, "yh", swaps[k])
            owned = owned + part.astype(f32) * float(far)

    (query_grad,) = call(
        query_kernel,
        [((query_count, width), f32)],
        [pltpu.VMEM((named_rows, width), bf16)],
        8 * product * (pool_rows + named_rows),
        pool_hi,
        pool_lo,
        named_hi,
        named_lo,
        named,
        *slabs,
        after=(rows_x,),
    )

    (summed,) = call(
        gather_sum_kernel,
        [((wide, tiles, SUBS, LANES), f32)],
        [pltpu.VMEM((wide, SUBS, LANES), f32)] * tiles,
        0,
        run,
        owners,
        back.astype(f32),
        smem=2,
    )
    with jax.named_scope("pieces_home"):
        home = lax.all_to_all(summed.astype(half), WIDE, 0, 0, tiled=True)
    home = home.reshape(runs, row_tiles, col_tiles, SUBS, LANES).transpose(0, 1, 3, 2, 4)
    home = home.reshape(runs * block_rows, width)
    returned = home[:block_rows].astype(f32)
    for r in range(1, runs):
        returned = returned + home[r * block_rows : (r + 1) * block_rows].astype(f32)
    return (query_grad, owned * (1.0 / LIFT) + returned * (1.0 / (LIFT * DROP)))


def solution(mesh):
    whole = Mesh(mesh.devices.reshape(4, 3, 2, 2, 4, 4), AXES)
    spec = P(AXES, None)
    return jax.shard_map(
        local,
        mesh=whole,
        in_specs=(spec, spec, P(AXES), spec),
        out_specs=(spec, spec),
        check_vma=False,
    )
```

```python
import functools
import math

import jax
import jax.numpy as jnp
from jax import lax
from jax.experimental import pallas as pl
from jax.experimental.pallas import tpu as pltpu
from jax.sharding import Mesh
from jax.sharding import PartitionSpec as P

AXES = ("zs", "zl", "yl", "c", "x", "yh")
WIDE = ("zs", "zl", "yl", "c")
RUN = ("zl", "yl", "c")
LANES = 128
SUBS = 8
LIFT = 128.0
DROP = 1.0 / 16.0
VMEM = 16 * 1024 * 1024
STEP = 256


def dot_nt(a, b):
    return lax.dot_general(a, b, (((1,), (1,)), ((), ())), preferred_element_type=jnp.float32)


def dot_tn(a, b):
    return lax.dot_general(a, b, (((0,), (0,)), ((), ())), preferred_element_type=jnp.float32)


def dot_nn(a, b):
    return lax.dot_general(a, b, (((1,), (0,)), ((), ())), preferred_element_type=jnp.float32)


def join_pieces(named_ref, keys_ref, row_tiles, col_tiles):
    rows = named_ref.shape[1]
    for r in range(row_tiles):
        for c in range(col_tiles):
            keys_ref[r * rows : (r + 1) * rows, c * LANES : (c + 1) * LANES] = named_ref[r * col_tiles + c]


def pick_kernel(run_ref, owners_ref, held_ref, out_ref):
    members, tiles, count = out_ref.shape[:3]
    stride = held_ref.shape[0] // (owners_ref.shape[0] // count)

    first = run_ref[0] * members
    for i in range(members):
        for k in range(count):
            owner = owners_ref[(first + i) * count + k]
            for u in range(tiles):
                out_ref[i, u, k] = held_ref[owner * stride + u]


def gather_sum_kernel(run_ref, owners_ref, terms_ref, out_ref, *acc_refs):
    members, tiles, count = terms_ref.shape[:3]
    for u in range(tiles):
        acc_refs[u][...] = jnp.zeros_like(acc_refs[u])

    first = run_ref[0] * members
    for i in range(members):
        for k in range(count):
            owner = owners_ref[(first + i) * count + k]
            for u in range(tiles):
                acc_refs[u][owner] += terms_ref[i, u, k]
    for u in range(tiles):
        out_ref[:, u] = acc_refs[u][...] * DROP


def pool_kernel(q_ref, *refs):
    slab_refs, (exp_ref, stat_ref) = refs[:-2], refs[-2:]
    width = q_ref.shape[1]
    step = slab_refs[0].shape[0]
    scaling = 4.0 / math.sqrt(width)
    q = q_ref[...]
    top = None
    for slot, slab_ref in enumerate(slab_refs):
        part = dot_nt(q, slab_ref[...]) * scaling
        exp_ref[:, slot * step : (slot + 1) * step] = part
        high = jnp.max(part, axis=-1, keepdims=True)
        top = high if top is None else jnp.maximum(top, high)
    total = jnp.zeros_like(top)
    for slot in range(len(slab_refs)):
        part = jnp.exp(exp_ref[:, slot * step : (slot + 1) * step] - top)
        exp_ref[:, slot * step : (slot + 1) * step] = part
        total += jnp.sum(part, axis=-1, keepdims=True)
    stat_ref[:, :LANES] = jnp.broadcast_to(top, (q.shape[0], LANES))
    stat_ref[:, LANES : 2 * LANES] = jnp.broadcast_to(total, (q.shape[0], LANES))
    stat_ref[:, 2 * LANES :] = q.astype(jnp.float32)


def split(grad):
    hi = grad.astype(jnp.bfloat16)
    return hi, (grad - hi.astype(jnp.float32)).astype(jnp.bfloat16)


def named_kernel(named_ref, stat_ref, hi_ref, lo_ref, named_out, share_ref, keys_ref, l_ref):
    width = keys_ref.shape[1]
    col_tiles = width // LANES
    row_tiles = named_ref.shape[0] // col_tiles
    piece_rows = named_ref.shape[1]
    named_rows = row_tiles * piece_rows
    scaling = 4.0 / math.sqrt(width)
    join_pieces(named_ref, keys_ref, row_tiles, col_tiles)
    q = stat_ref[:, 2 * LANES :].astype(jnp.bfloat16)
    pool_top = stat_ref[:, :1]
    top = pool_top
    for c in range(0, named_rows, STEP):
        part = dot_nt(q, keys_ref[c : c + STEP, :]) * scaling
        l_ref[:, c : c + STEP] = part
        top = jnp.maximum(top, jnp.max(part, axis=-1, keepdims=True))
    pool_scale = jnp.exp(pool_top - top)
    total = stat_ref[:, LANES : LANES + 1] * pool_scale
    for c in range(0, named_rows, STEP):
        part = jnp.exp(l_ref[:, c : c + STEP] - top)
        l_ref[:, c : c + STEP] = part
        total += jnp.sum(part, axis=-1, keepdims=True)
    share = 1.0 / total
    share_ref[...] = jnp.broadcast_to(share * pool_scale, share_ref.shape)
    for c in range(0, named_rows, STEP):
        hi, lo = split(l_ref[:, c : c + STEP] * share)
        hi_ref[:, c : c + STEP] = hi
        lo_ref[:, c : c + STEP] = lo
        terms = (dot_tn(hi, q) + dot_tn(lo, q)) * (scaling * LIFT)
        first = c // piece_rows
        for r in range(STEP // piece_rows):
            for k in range(col_tiles):
                named_out[(first + r) * col_tiles + k] = terms[
                    r * piece_rows : (r + 1) * piece_rows, k * LANES : (k + 1) * LANES
                ]


def pool_grad_kernel(place_ref, q_ref, exp_ref, share_ref, pos_ref, hi_ref, lo_ref, *grad_refs):
    queries, width = q_ref.shape
    step = grad_refs[0].shape[0]
    scaling = 4.0 / math.sqrt(width)
    q = q_ref[...]
    share = share_ref[:, :1]
    across = lax.broadcasted_iota(jnp.int32, (queries, queries), 1)
    down = lax.broadcasted_iota(jnp.int32, (queries, queries), 0)
    pos = jnp.sum(jnp.where(across == down, pos_ref[...].astype(jnp.float32), 0.0), axis=1, keepdims=True)
    pos = pos.astype(jnp.int32)
    block = step // place_ref.shape[0]
    for slot, grad_ref in enumerate(grad_refs):
        first, last = slot * step, (slot + 1) * step
        columns = lax.broadcasted_iota(jnp.int32, (queries, step), 1) + first
        hi, lo = split(exp_ref[:, first:last] * share - (columns == pos).astype(jnp.float32))
        hi_ref[:, first:last] = hi
        lo_ref[:, first:last] = lo
        terms = (dot_tn(hi, q) + dot_tn(lo, q)) * (scaling * LIFT)
        for r in range(step // block):
            grad_ref[pl.ds(pl.multiple_of(place_ref[r] * block, block), block), :] = terms[r * block : (r + 1) * block]


def query_kernel(pool_hi_ref, pool_lo_ref, hi_ref, lo_ref, named_ref, *refs):
    slab_refs, out_ref, keys_ref = refs[:-2], refs[-2], refs[-1]
    step, width = slab_refs[0].shape
    col_tiles = width // LANES
    row_tiles = named_ref.shape[0] // col_tiles
    scaling = 4.0 / math.sqrt(width)
    join_pieces(named_ref, keys_ref, row_tiles, col_tiles)
    total = dot_nn(hi_ref[...], keys_ref[...]) + dot_nn(lo_ref[...], keys_ref[...])
    for slot, slab_ref in enumerate(slab_refs):
        first, last = slot * step, (slot + 1) * step
        total += dot_nn(pool_hi_ref[:, first:last], slab_ref[...])
        total += dot_nn(pool_lo_ref[:, first:last], slab_ref[...])
    out_ref[...] = total * scaling


def call(kernel, outs, scratch, flops, *args, smem=0, after=()):
    vmem = pl.BlockSpec(memory_space=pltpu.VMEM)
    specs = [pl.BlockSpec(memory_space=pltpu.SMEM)] * smem + [vmem] * (len(args) - smem)
    specs += [pl.BlockSpec(memory_space=pltpu.HBM)] * len(after)
    count = len(args)

    def body(*refs):
        kernel(*refs[:count], *refs[count + len(after) :])

    return pl.pallas_call(
        body,
        out_shape=tuple(jax.ShapeDtypeStruct(shape, dtype) for shape, dtype in outs),
        in_specs=specs,
        out_specs=(vmem,) * len(outs),
        scratch_shapes=scratch,
        compiler_params=pltpu.CompilerParams(vmem_limit_bytes=VMEM),
        cost_estimate=pl.CostEstimate(flops=flops, bytes_accessed=4 * 1024 * 1024, transcendentals=0),
    )(*args, *after)


def local(queries, passages, positive, negative_owners):
    query_count, width = queries.shape
    block_rows = passages.shape[0]
    neg_count = negative_owners.shape[1]
    f32, bf16, half = jnp.float32, jnp.bfloat16, jnp.float16
    wide, members, runs = lax.axis_size(WIDE), lax.axis_size(RUN), lax.axis_size("zs")
    near, far = lax.axis_size("yh"), lax.axis_size("x")
    row_tiles, col_tiles = block_rows // SUBS, width // LANES
    tiles = row_tiles * col_tiles // members
    pool_rows = far * near * block_rows
    named_rows = neg_count * block_rows
    swaps = [[(i, i ^ k) for i in range(near)] for k in range(near)]
    here_x, here_y = lax.axis_index("x"), lax.axis_index("yh")
    run = lax.axis_index("zs").astype(jnp.int32)[None]

    pieces = passages.reshape(row_tiles, SUBS, col_tiles, LANES).transpose(0, 2, 1, 3)
    pieces = pieces.reshape(members, tiles * SUBS, LANES)
    names = jnp.pad(negative_owners[0].astype(bf16), (0, LANES - neg_count))
    rows = tiles * SUBS
    shape = (runs, members, rows + SUBS, LANES)
    row = lax.broadcasted_iota(jnp.int32, shape, 2)
    sent = jnp.pad(pieces, ((0, 0), (0, SUBS), (0, 0)))
    sent = jnp.where(row < rows, jnp.broadcast_to(sent[None], shape), jnp.broadcast_to(names, shape))
    sent = sent.reshape(wide, rows + SUBS, LANES)
    with jax.named_scope("spread_pieces"):
        spread = lax.all_to_all(sent, WIDE, 0, 0, tiled=True)
    owners = spread[:, tiles * SUBS, :neg_count].astype(jnp.int32).reshape(wide * neg_count)

    with jax.named_scope("pool_yh"):
        mine = lax.all_gather(passages, "yh", axis=0, tiled=True)
    with jax.named_scope("pool_x"):
        slabs = [mine] + [lax.ppermute(mine, "x", swaps[k]) for k in range(1, far)]
    slots = positive ^ (here_x * (near * block_rows))

    (picked,) = call(
        pick_kernel,
        [((members, tiles, neg_count, SUBS, LANES), bf16)],
        [],
        0,
        run,
        owners,
        spread.reshape(wide * (tiles + 1), SUBS, LANES),
        smem=2,
        after=(mine,),
    )
    with jax.named_scope("named_pieces"):
        named = lax.all_to_all(picked, RUN, 0, 0, tiled=True)
    named = named.reshape(members * tiles, neg_count * SUBS, LANES)

    product = 2 * query_count * width
    exps, stats = call(
        pool_kernel,
        [((query_count, pool_rows), f32), ((query_count, 2 * LANES + width), f32)],
        [],
        100 * product * pool_rows,
        queries,
        *slabs,
    )
    named_hi, named_lo, named_grad, share = call(
        named_kernel,
        [
            ((query_count, named_rows), bf16),
            ((query_count, named_rows), bf16),
            ((members * tiles, neg_count * SUBS, LANES), f32),
            ((query_count, LANES), f32),
        ],
        [pltpu.VMEM((named_rows, width), bf16), pltpu.VMEM((query_count, named_rows), f32)],
        3 * product * named_rows,
        named,
        stats,
    )
    with jax.named_scope("named_back"):
        back = named_grad.astype(half).reshape(members, tiles, neg_count, SUBS, LANES)
        back = lax.all_to_all(back, RUN, 0, 0, tiled=True)

    pool_hi, pool_lo, *pool_grads = call(
        pool_grad_kernel,
        [((query_count, pool_rows), bf16)] * 2 + [((near * block_rows, width), f32)] * far,
        [],
        2 * product * pool_rows,
        jnp.arange(near, dtype=jnp.int32) ^ here_y.astype(jnp.int32),
        queries,
        exps,
        share,
        slots[None, :],
        smem=1,
    )
    rows_x = pool_grads[0]
    leaving = [grad.astype(half) for grad in pool_grads[1:]]
    with jax.named_scope("grad_x"):
        for k in range(1, far):
            part = lax.ppermute(leaving[k - 1], "x", swaps[k])
            rows_x = rows_x + part.astype(f32)
    owned = rows_x[:block_rows]
    with jax.named_scope("grad_yh"):
        for k in (2, 1, 3):
            part = (rows_x[k * block_rows : (k + 1) * block_rows] * (1.0 / far)).astype(half)
            part = lax.ppermute(part, "yh", swaps[k])
            owned = owned + part.astype(f32) * float(far)

    (query_grad,) = call(
        query_kernel,
        [((query_count, width), f32)],
        [pltpu.VMEM((named_rows, width), bf16)],
        8 * product * (pool_rows + named_rows),
        pool_hi,
        pool_lo,
        named_hi,
        named_lo,
        named,
        *slabs,
        after=(rows_x,),
    )

    (summed,) = call(
        gather_sum_kernel,
        [((wide, tiles, SUBS, LANES), f32)],
        [pltpu.VMEM((wide, SUBS, LANES), f32)] * tiles,
        0,
        run,
        owners,
        back.astype(f32),
        smem=2,
    )
    with jax.named_scope("pieces_home"):
        home = lax.all_to_all(summed.astype(half), WIDE, 0, 0, tiled=True)
    home = home.reshape(runs, row_tiles, col_tiles, SUBS, LANES).transpose(0, 1, 3, 2, 4)
    home = home.reshape(runs * block_rows, width)
    returned = home[:block_rows].astype(f32)
    for r in range(1, runs):
        returned = returned + home[r * block_rows : (r + 1) * block_rows].astype(f32)
    return (query_grad, owned * (1.0 / LIFT) + returned * (1.0 / (LIFT * DROP)))


def solution(mesh):
    whole = Mesh(mesh.devices.reshape(4, 3, 2, 2, 4, 4), AXES)
    spec = P(AXES, None)
    return jax.shard_map(
        local,
        mesh=whole,
        in_specs=(spec, spec, P(AXES), spec),
        out_specs=(spec, spec),
        check_vma=False,
    )
```
